512 devices in a mesh: dp: 64 (over x_hi, z, core), tensor: 8 (over y, x_lo).
Axes of the slice: x: 4 (x_hi: 2, x_lo: 2; x = x_hi * 2 + x_lo), y: 4, z: 16, core: 2. Of those that a mesh axis runs over, the one named last changes fastest.
Arguments:
- out_grads: bfloat16 [3, 4, 8192, 8192], P(None, None, 'dp', 'tensor'), may hold values from -8 to 8
- grad_w: bfloat16 [4, 2048, 8192], P(None, 'dp', 'tensor'), may hold values from -122 to 122
- factor_avg: float32 [512, 64, 64], P(('dp', 'tensor')), may hold values from -1 to 1, as said below
- owner_table: int32 [64], replicated, may hold values from 0 to 63, each once
Outputs:
- update: bfloat16 [4, 2048, 8192], P(None, 'dp', 'tensor')
- fresh: float32 [512, 64, 64], P(('dp', 'tensor'))
The draws below stay inside these ranges and needn't reach their ends.
Inputs may be any that keep to these rules, and one draw needn't show every extreme that they name: `owner_table`: each block index appears once. `factor_avg`: each block is symmetric with a positive diagonal larger than the sum of magnitudes of its row's other entries.
All inputs are finite; a program needn't handle non-finite values. Where the reference program divides by a largest or mean magnitude, that divisor is 1e-20 or more.
Results may differ from the reference program's by a relative error of at most 0.0044.
The reference program's roundings to bfloat16 on the way (of `inverse_half` and `precond`) count: a program that leaves them out, or rounds other values in their place, can miss the bound.
Values may be sent and summed in bfloat16 or wider, within the bound.
A program may use at most 64 MiB of HBM per device.

```python
import math
import jax
import jax.numpy as jnp
from jax import lax

D = 2048
FF = 8192
BLOCK = 64
LAYERS = 4
REFRESH = 3
STEPS = 8
TOKENS = 8192
NBLK = 512
NBT = 64
CAP = 1
N_DP = 64
N_TENSOR = 8


def draw_out_grads(key, part):
    key = jax.random.fold_in(key, 1)
    first, second = jax.random.split(key, 2)
    shape = (REFRESH, LAYERS, TOKENS, FF)
    scales = jnp.exp(jax.random.uniform(first, (LAYERS, FF), minval=math.log(0.05), maxval=0.0))
    noise = jnp.clip(jax.random.normal(second, shape), -5.0, 5.0)
    mixed = noise + 0.6 * jnp.roll(noise, 1, axis=3)
    return (mixed * scales[None, :, None, :]).astype(jnp.bfloat16)


def draw_grad_w(key, part):
    key = jax.random.fold_in(key, 3)
    first, second, third = jax.random.split(key, 3)
    row_rough = jnp.exp(jax.random.uniform(first, (LAYERS, D), minval=0.0, maxval=math.log(4.0)))
    col_rough = jnp.exp(jax.random.uniform(second, (LAYERS, FF), minval=0.0, maxval=math.log(4.0)))
    cols_up = 3.0 ** (jnp.arange(FF, dtype=jnp.float32) / FF)
    rows_up = 3.0 ** (jnp.arange(D, dtype=jnp.float32) / D)
    noise = jnp.clip(jax.random.normal(third, (LAYERS, D, FF)), -5.0, 5.0)
    row_scale = rows_up[None, :] * row_rough
    col_scale = cols_up[None, :] * col_rough
    return (noise * row_scale[:, :, None] * col_scale[:, None, :] / 6.0).astype(jnp.bfloat16)


def draw_factor_avg(key, part):
    key = jax.random.fold_in(key, 2)
    first, second = jax.random.split(key)
    diagonal = jnp.exp(jax.random.uniform(first, (NBLK, BLOCK), minval=math.log(0.003), maxval=0.0))
    rough = jax.random.uniform(second, (NBLK, BLOCK, BLOCK), minval=-1.0, maxval=1.0)
    rough = 0.5 * (rough + jnp.swapaxes(rough, 1, 2))
    bound = jnp.minimum(diagonal[:, :, None], diagonal[:, None, :]) * (0.9 / BLOCK)
    identity = jnp.eye(BLOCK, dtype=jnp.float32)
    return diagonal[:, :, None] * identity + (1.0 - identity) * rough * bound


def setup_inputs(seed: int = 0) -> dict:
    seeds = jax.random.split(jax.random.key(seed), 5)
    return {
        "out_grads": draw_out_grads(jax.random.fold_in(seeds[4], 71), 0),
        "grad_w": draw_grad_w(jax.random.fold_in(seeds[4], 71), 0),
        "factor_avg": draw_factor_avg(jax.random.fold_in(seeds[4], 71), 0),
        "owner_table": jax.random.permutation(seeds[3], NBT).astype(jnp.int32),
    }


average_decay = 0.75
damping = 0.003
kl_clip = 0.1

def newton_schulz(damped):
    identity = jnp.eye(damped.shape[-1], dtype=jnp.float32)
    scale = 1.0 / lax.optimization_barrier(jnp.max(lax.optimization_barrier(jnp.sum(jnp.abs(damped), axis=2)), axis=1))
    inverse = scale[:, None, None] * identity
    for _ in range(STEPS):
        product = jnp.matmul(damped, inverse, precision=lax.Precision.HIGHEST)
        inverse = jnp.matmul(inverse, 2.0 * identity - product, precision=lax.Precision.HIGHEST)
    return inverse

def reference(out_grads, grad_w, factor_avg, owner_table):
    per_rank = FF // N_TENSOR
    per_layer = per_rank // BLOCK
    weights = [(1.0 - average_decay) * average_decay ** (REFRESH - 1 - turn) / TOKENS for turn in range(REFRESH)]

    def gram_of_slot(index):
        owner = index // (N_TENSOR * CAP)
        tensor_rank = index // CAP % N_TENSOR
        local = owner * CAP + index % CAP
        block_id = owner_table[local]
        layer = (block_id // per_layer).astype(jnp.int32)
        column = (tensor_rank * per_rank + block_id % per_layer * BLOCK).astype(jnp.int32)
        zero = jnp.zeros((), jnp.int32)
        portion = lax.dynamic_slice(out_grads, (zero, layer, zero, column), (REFRESH, 1, TOKENS, BLOCK))
        summed = jnp.zeros((BLOCK, BLOCK), jnp.float32)
        for turn in range(REFRESH):
            rows_here = portion[turn, 0]
            summed = summed + weights[turn] * jnp.dot(rows_here.T, rows_here, preferred_element_type=jnp.float32)
        return summed
    grams = lax.map(gram_of_slot, jnp.arange(NBLK, dtype=jnp.int32))
    fresh = average_decay ** REFRESH * factor_avg + grams
    identity = jnp.eye(BLOCK, dtype=jnp.float32)
    inverse = newton_schulz(fresh + damping * identity)
    inverse_half = inverse.astype(jnp.bfloat16)
    slot_of = jnp.argsort(owner_table).astype(jnp.int32)
    by_rank = inverse_half.reshape(N_DP, N_TENSOR, CAP, BLOCK, BLOCK).transpose(1, 0, 2, 3, 4)
    by_rank = by_rank.reshape(N_TENSOR, NBT, BLOCK, BLOCK)
    by_block = by_rank[:, slot_of].reshape(N_TENSOR, LAYERS, per_layer, BLOCK, BLOCK)
    grads_split = grad_w.reshape(LAYERS, D, N_TENSOR, per_layer, BLOCK).astype(jnp.float32)
    precond = jnp.einsum('ldtjb,tljbc->ldtjc', grads_split, by_block.astype(jnp.float32), precision=lax.Precision.HIGHEST)
    precond = precond.reshape(LAYERS, D, FF).astype(jnp.bfloat16)
    inner = jnp.sum(grad_w.astype(jnp.float32) * precond.astype(jnp.float32))
    clip = jnp.minimum(1.0, jnp.sqrt(kl_clip * float(LAYERS * D * FF) / inner))
    update = (clip * precond.astype(jnp.float32)).astype(jnp.bfloat16)
    return (update, fresh)
```

```python
import functools

import jax
import jax.numpy as jnp
from jax import lax
from jax.experimental import pallas as pl
from jax.experimental.pallas import tpu as pltpu
from jax.sharding import PartitionSpec as P

STEPS = 8
AVERAGE_DECAY = 0.75
DAMPING = 0.003
KL_CLIP = 0.1
MESH = pl.DeviceIdType.MESH
F32 = jnp.float32
BF16 = jnp.bfloat16


def newton_schulz(damped):
    size = damped.shape[0]
    rows = lax.broadcasted_iota(jnp.int32, (size, size), 0)
    cols = lax.broadcasted_iota(jnp.int32, (size, size), 1)
    identity = jnp.where(rows == cols, 1.0, 0.0).astype(F32)
    scale = 1.0 / jnp.max(jnp.sum(jnp.abs(damped), axis=1, keepdims=True), axis=0, keepdims=True)
    error = identity - scale * damped
    inverse = scale * (identity + error)
    error = jnp.dot(error, error, precision=lax.Precision.HIGHEST, preferred_element_type=F32)
    for step in range(1, STEPS):
        if step < STEPS - 1:
            both = jnp.concatenate([error, inverse], axis=1)
            both = jnp.dot(error, both, precision=lax.Precision.HIGHEST, preferred_element_type=F32)
            inverse = inverse + both[:, size:]
            error = both[:, :size]
        else:
            inverse = inverse + jnp.dot(
                error, inverse, precision=lax.Precision.HIGHEST, preferred_element_type=F32
            )
    return inverse


def exchange_kernel(
    nz, nt, entries, table, og, gw, fa, pre_o, clip_o, fresh_o,
    ybuf, gbuf, fbuf, gram, gblk, mine, snd1, rcv1, snd2, rcv2, xs, xall, inn, tin, xin, cin,
    lsem, s1s, s1r, s2s, s2r, ags, agr, fws, ts, tr, xss, xsr, cs,
):
    refresh, layers, tokens, columns = ybuf.shape
    slots, half, _ = gram.shape
    size = 2 * half
    per_layer = columns // size
    chips = slots // 2
    dp = lax.axis_index("dp")
    t = lax.axis_index("tensor")
    core = lax.rem(dp, 2)
    me = lax.div(dp, 2)
    xh = lax.div(me, nz)
    z = lax.rem(me, nz)
    mate = (dp + 1 - 2 * core, t)

    def far(i):
        j = lax.div(i, 2)
        a = 1 - lax.rem(i, 2)
        k = nz // 2 + lax.div(j + 1, 2) * (1 - 2 * lax.rem(j, 2))
        return lax.rem(xh + a, 2) * nz + lax.rem(z + k, nz)

    others = chips - 1

    def loads():
        out = []
        for l in range(layers):
            for i in range(refresh):
                out.append(pltpu.make_async_copy(og.at[i, l], ybuf.at[i, l], lsem.at[l * refresh + i]))
        return out

    ycopies = loads()
    gcopy = pltpu.make_async_copy(gw, gbuf, lsem.at[layers * refresh])
    fcopy = pltpu.make_async_copy(fa, fbuf, lsem.at[layers * refresh + 1])
    for cp in ycopies[:refresh]:
        cp.start()

    barrier = pltpu.get_barrier_semaphore()

    def greet(i, carry):
        pl.semaphore_signal(barrier, inc=1, device_id=(far(i) * 2 + core, t), device_id_type=MESH)
        return carry

    lax.fori_loop(0, others, greet, 0)
    pl.semaphore_signal(barrier, inc=1, device_id=mate, device_id_type=MESH)
    for k in range(1, nt):
        pl.semaphore_signal(
            barrier, inc=1, device_id=(dp, lax.rem(t + k, nt)), device_id_type=MESH
        )
    for cp in ycopies[refresh:]:
        cp.start()
    gcopy.start()
    fcopy.start()

    weights = [
        (1.0 - AVERAGE_DECAY) * AVERAGE_DECAY ** (refresh - 1 - i) / entries[0] for i in range(refresh)
    ]
    for l in range(layers):
        for i in range(refresh):
            ycopies[l * refresh + i].wait()
        for p in range(per_layer // 2):
            total = None
            for i in range(refresh):
                y = ybuf[i, l, :, 2 * size * p : 2 * size * (p + 1)]
                part = weights[i] * lax.dot_general(
                    y, y, (((0,), (0,)), ((), ())), preferred_element_type=F32
                )
                total = part if total is None else total + part
            b = l * per_layer + 2 * p
            gram[b] = jnp.concatenate([total[:half, :size], total[half:size, :size]], axis=1)
            gram[b + 1] = jnp.concatenate(
                [total[size : size + half, size:], total[size + half :, size:]], axis=1
            )

    def order(q, carry):
        mine[q] = gram[table[2 * q + core]]
        snd1[q] = gram[table[2 * q + 1 - core]].astype(BF16)
        return carry

    lax.fori_loop(0, chips, order, 0)

    gcopy.wait()
    for l in range(layers):
        for j in range(per_layer):
            gblk[l * per_layer + j] = gbuf[l, :, size * j : size * (j + 1)]

    pl.semaphore_wait(barrier, others + nt)

    cp1 = pltpu.make_async_remote_copy(
        src_ref=snd1, dst_ref=rcv1, send_sem=s1s, recv_sem=s1r, device_id=mate, device_id_type=MESH
    )
    cp1.start()
    cp1.wait_recv()

    def scatter(q, slot):
        return pltpu.make_async_remote_copy(
            src_ref=snd2.at[q], dst_ref=rcv2.at[slot], send_sem=s2s.at[q], recv_sem=s2r.at[slot],
            device_id=(q * 2 + core, t), device_id_type=MESH,
        )

    def send_sums(i, carry):
        q = far(i)
        snd2[q] = (mine[q] + rcv1[q].astype(F32)).astype(BF16)
        scatter(q, me).start()
        return carry

    lax.fori_loop(0, others, send_sums, 0)

    def take_sums(i, acc):
        q = far(others - 1 - i)
        scatter(q, q).wait_recv()
        return acc + rcv2[q].astype(F32)

    grams = lax.fori_loop(0, others, take_sums, mine[me] + rcv1[me].astype(F32))
    grams = jnp.concatenate([grams[:, :size], grams[:, size:]], axis=0)
    fcopy.wait()
    fresh = AVERAGE_DECAY**refresh * fbuf[0] + grams
    fresh_o[0] = fresh
    rows = lax.broadcasted_iota(jnp.int32, (size, size), 0)
    cols = lax.broadcasted_iota(jnp.int32, (size, size), 1)
    inverse = newton_schulz(fresh + jnp.where(rows == cols, DAMPING, 0.0))
    packed = jnp.concatenate([inverse[:half], inverse[half:]], axis=1).astype(BF16)
    xs[...] = packed
    xall[core, me] = packed

    def gather(q, slot):
        return pltpu.make_async_remote_copy(
            src_ref=xs, dst_ref=xall.at[core, slot], send_sem=ags.at[q], recv_sem=agr.at[core, slot],
            device_id=(q * 2 + core, t), device_id_type=MESH,
        )

    def forward(q, owner):
        return pltpu.make_async_remote_copy(
            src_ref=xall.at[core, q], dst_ref=xall.at[owner, q], send_sem=fws.at[q],
            recv_sem=agr.at[owner, q], device_id=mate, device_id_type=MESH,
        )

    def send_inverse(i, carry):
        gather(far(i), me).start()
        return carry

    lax.fori_loop(0, others, send_inverse, 0)
    forward(me, core).start()

    def apply(owner, q, acc):
        x = xall[owner, q]
        top, bottom = x[:, :size], x[:, size:]
        x2 = jnp.concatenate(
            [jnp.concatenate([top, top], axis=1), jnp.concatenate([bottom, bottom], axis=1)], axis=0
        )
        g = gblk[table[2 * q + owner]]
        out = jnp.dot(g, x2, preferred_element_type=F32).astype(BF16)
        pre_o[2 * q + owner] = out
        return acc + g.astype(F32) * out[:, :size].astype(F32)

    def take_direct(i, acc):
        q = far(others - 1 - i)
        gather(q, q).wait_recv()
        forward(q, core).start()
        return apply(core, q, acc)

    acc = apply(core, me, jnp.zeros((gbuf.shape[1], size), F32))
    acc = lax.fori_loop(0, others, take_direct, acc)

    def take_forwarded(q, acc):
        forward(q, 1 - core).wait_recv()
        return apply(1 - core, q, acc)

    acc = lax.fori_loop(0, chips, take_forwarded, acc)

    local = jnp.sum(acc, axis=0, keepdims=True)
    local = jnp.concatenate([local, jnp.zeros_like(local)], axis=1)
    inn[0] = local
    tcopies = []
    for k in range(1, nt):
        cp = pltpu.make_async_remote_copy(
            src_ref=inn.at[0], dst_ref=tin.at[k], send_sem=ts.at[k], recv_sem=tr.at[k],
            device_id=(dp, lax.rem(t + k, nt)), device_id_type=MESH,
        )
        cp.start()
        tcopies.append(cp)
    total = local
    for k in range(1, nt):
        tcopies[k - 1].wait_recv()
        total = total + tin[k]
    inn[1] = total

    def spread(q, slot):
        return pltpu.make_async_remote_copy(
            src_ref=inn.at[1], dst_ref=xin.at[slot], send_sem=xss.at[q], recv_sem=xsr.at[slot],
            device_id=(q * 2 + core, t), device_id_type=MESH,
        )

    def send_inner(i, carry):
        spread(far(i), me).start()
        return carry

    lax.fori_loop(0, others, send_inner, 0)

    def take_inner(i, acc):
        q = far(others - 1 - i)
        spread(q, q).wait_recv()
        return acc + xin[q]

    total = lax.fori_loop(0, others, take_inner, total)
    inn[2] = total
    ccopy = pltpu.make_async_remote_copy(
        src_ref=inn.at[2], dst_ref=cin, send_sem=cs.at[0], recv_sem=cs.at[1],
        device_id=mate, device_id_type=MESH,
    )
    ccopy.start()
    ccopy.wait_recv()
    inner = jnp.sum(total + cin[...], axis=1, keepdims=True)
    clip = jnp.minimum(1.0, jnp.sqrt(KL_CLIP * entries[1] / inner))
    clip_o[...] = jnp.broadcast_to(clip, clip_o.shape)

    cp1.wait_send()
    ccopy.wait_send()
    for cp in tcopies:
        cp.wait_send()

    def drain(i, carry):
        q = far(i)
        scatter(q, me).wait_send()
        gather(q, me).wait_send()
        spread(q, me).wait_send()
        forward(q, core).wait_send()
        return carry

    lax.fori_loop(0, others, drain, 0)
    forward(me, core).wait_send()


def finish_kernel(table, pre, clip, fresh, update, fresh_o, slot_of):
    layers, rows, columns = update.shape
    slots = pre.shape[0]
    width = pre.shape[2]
    pairs = columns // width
    fresh_o[...] = fresh[...]

    def invert(r, carry):
        slot_of[table[r]] = r
        return carry

    lax.fori_loop(0, slots, invert, 0)
    factor = clip[0:1, :]
    left = lax.broadcasted_iota(jnp.int32, (rows, width), 1) < width // 2
    for l in range(layers):
        for p in range(pairs):
            b = (l * pairs + p) * 2
            both = jnp.where(left, pre[slot_of[b]].astype(F32), pre[slot_of[b + 1]].astype(F32))
            update[l, :, p * width : (p + 1) * width] = (factor * both).astype(BF16)


def shards(out_grads, grad_w, factor_avg, owner_table):
    refresh, layers, tokens, columns = out_grads.shape
    _, size, _ = factor_avg.shape
    rows = grad_w.shape[1]
    slots = owner_table.shape[0]
    half = size // 2
    n_dp = lax.axis_size("dp")
    nt = lax.axis_size("tensor")
    nz = n_dp // 4
    chips = slots // 2
    entries = (float(tokens * n_dp), float(layers * rows * n_dp * columns * nt))
    dma = pltpu.SemaphoreType.DMA
    hbm = pl.BlockSpec(memory_space=pltpu.HBM)
    vmem = pl.BlockSpec(memory_space=pltpu.VMEM)
    smem = pl.BlockSpec(memory_space=pltpu.SMEM)
    pre, clip, fresh = pl.pallas_call(
        functools.partial(exchange_kernel, nz, nt, entries),
        out_shape=(
            jax.ShapeDtypeStruct((slots, rows, 2 * size), BF16),
            jax.ShapeDtypeStruct((8, 2 * size), F32),
            jax.ShapeDtypeStruct(factor_avg.shape, F32),
        ),
        in_specs=[smem, hbm, hbm, hbm],
        out_specs=(vmem, vmem, vmem),
        scratch_shapes=[
            pltpu.VMEM(out_grads.shape, BF16),
            pltpu.VMEM(grad_w.shape, BF16),
            pltpu.VMEM(factor_avg.shape, F32),
            pltpu.VMEM((slots, half, 2 * size), F32),
            pltpu.VMEM((slots, rows, size), BF16),
            pltpu.VMEM((chips, half, 2 * size), F32),
            pltpu.VMEM((chips, half, 2 * size), BF16),
            pltpu.VMEM((chips, half, 2 * size), BF16),
            pltpu.VMEM((chips, half, 2 * size), BF16),
            pltpu.VMEM((chips, half, 2 * size), BF16),
            pltpu.VMEM((half, 2 * size), BF16),
            pltpu.VMEM((2, chips, half, 2 * size), BF16),
            pltpu.VMEM((3, 1, 2 * size), F32),
            pltpu.VMEM((nt, 1, 2 * size), F32),
            pltpu.VMEM((chips, 1, 2 * size), F32),
            pltpu.VMEM((1, 2 * size), F32),
            dma((layers * refresh + 2,)),
            dma,
            dma,
            dma((chips,)),
            dma((chips,)),
            dma((chips,)),
            dma((2, chips)),
            dma((chips,)),
            dma((nt,)),
            dma((nt,)),
            dma((chips,)),
            dma((chips,)),
            dma((2,)),
        ],
        compiler_params=pltpu.CompilerParams(
            collective_id=0, has_side_effects=True, vmem_limit_bytes=48 * 2**20
        ),
        name="exchange",
    )(owner_table, out_grads, grad_w, factor_avg)
    return pl.pallas_call(
        finish_kernel,
        out_shape=(
            jax.ShapeDtypeStruct(grad_w.shape, BF16),
            jax.ShapeDtypeStruct(factor_avg.shape, F32),
        ),
        in_specs=[smem, vmem, vmem, vmem],
        out_specs=(vmem, vmem),
        scratch_shapes=[pltpu.SMEM((slots,), jnp.int32)],
        compiler_params=pltpu.CompilerParams(vmem_limit_bytes=16 * 2**20),
        name="finish",
    )(owner_table, pre, clip, fresh)


def solution(mesh):
    placed = (
        P(None, None, "dp", "tensor"),
        P(None, "dp", "tensor"),
        P(("dp", "tensor"), None, None),
        P(),
    )
    return jax.shard_map(
        shards,
        mesh=mesh,
        in_specs=placed,
        out_specs=(P(None, "dp", "tensor"), P(("dp", "tensor"), None, None)),
        check_vma=False,
    )
```

```python
import functools

import jax
import jax.numpy as jnp
from jax import lax
from jax.experimental import pallas as pl
from jax.experimental.pallas import tpu as pltpu
from jax.sharding import PartitionSpec as P

STEPS = 8
AVERAGE_DECAY = 0.75
DAMPING = 0.003
KL_CLIP = 0.1
MESH = pl.DeviceIdType.MESH
F32 = jnp.float32
BF16 = jnp.bfloat16


def iota(shape, axis):
    return lax.broadcasted_iota(jnp.int32, shape, axis)


def newton_schulz(damped):
    size = damped.shape[0]
    identity = jnp.where(iota((size, size), 0) == iota((size, size), 1), 1.0, 0.0).astype(F32)

    def dot(a, b):
        return jnp.dot(a, b, precision=lax.Precision.HIGHEST, preferred_element_type=F32)

    scale = 1.0 / jnp.max(jnp.sum(jnp.abs(damped), axis=1, keepdims=True), axis=0, keepdims=True)
    error = identity - scale * damped
    inverse = scale * (identity + error)
    for _ in range(1, STEPS):
        error = dot(error, error)
        inverse = inverse + dot(error, inverse)
    return inverse


def pack_pair(total, body, diag, b):
    wide = total.shape[0]
    size, half, quarter = wide // 2, wide // 4, wide // 8
    row, lane = iota((half, wide), 0), iota((half, wide), 1)
    first = lane < size
    local = jnp.where(first, lane, lane - size)
    upper = jnp.where(first, total[:half], total[size : size + half])
    lower = jnp.where(first, total[half:size], total[size + half :])
    moved = pltpu.roll(lower, wide - half, 1)
    both = jnp.where((local < half) & (row > local), moved, upper)
    turned = pltpu.roll(both, size, 1)
    side = iota((quarter, wide), 1) < size
    body[b] = jnp.where(side, both[:quarter], turned[quarter:])
    body[b + 1] = jnp.where(side, turned[:quarter], both[quarter:])
    on = jnp.where(row == local, upper, 0.0) + jnp.where(row + half == local, lower, 0.0)
    on = jnp.sum(on, axis=0, keepdims=True)
    swapped = pltpu.roll(on, size, 1)
    side = iota((1, wide), 1) < size
    diag[b] = jnp.where(side, on, swapped)
    diag[b + 1] = jnp.where(side, swapped, on)


def unpack(body, diag):
    quarter, wide = body.shape
    size, half = wide // 2, wide // 4
    rows = jnp.concatenate([body[:, :size], body[:, size:]], axis=0)
    corner, side = rows[:, :half], rows[:, half:]
    turned = corner.T
    row, col = iota((half, half), 0), iota((half, half), 1)
    first = jnp.where(col > row, corner, turned)
    last = jnp.where(col < row, corner, turned)
    whole = jnp.concatenate(
        [jnp.concatenate([first, side], axis=1), jnp.concatenate([side.T, last], axis=1)], axis=0
    )
    return jnp.where(iota((size, size), 0) == iota((size, size), 1), diag[:, :size], whole)


def pack_one(whole):
    size = whole.shape[0]
    half, quarter = size // 2, size // 4
    row, col = iota((half, half), 0), iota((half, half), 1)
    corner = jnp.where(row > col, whole[half:, half:], whole[:half, :half])
    rows = jnp.concatenate([corner, whole[:half, half:]], axis=1)
    body = jnp.concatenate([rows[:quarter], rows[quarter:]], axis=1)
    on = jnp.where(iota((size, size), 0) == iota((size, size), 1), whole, 0.0)
    on = jnp.sum(on, axis=0, keepdims=True)
    return body, jnp.concatenate([on, on], axis=1)


def exchange_kernel(
    nz, nt, entries, table, og, gw, fa, update_o, fresh_o,
    ybuf, gbuf, fbuf, gram, dgram, hess, dhess, pos_v, pos,
    amine, asend, arecv, asum, agot, admine, adsend, adrecv, adsum, adgot,
    hmine, hsend, hrecv, hsum, hgot, hdmine, hdsend, hdrecv, hdsum, hdgot,
    xs, xd, xall, xdall, inn, tin, xin, cin, lsem, ssem, rsem,
):
    refresh, layers, tokens, columns = ybuf.shape
    slots, quarter, wide = gram.shape
    size = wide // 2
    per_layer = columns // size
    chips = slots // 2
    others = chips - 1
    dp = lax.axis_index("dp")
    t = lax.axis_index("tensor")
    core = lax.rem(dp, 2)
    here = lax.div(dp, 2)
    xh = lax.div(here, nz)
    z = lax.rem(here, nz)
    mate = (dp + 1 - 2 * core, t)

    copies = [
        [pltpu.make_async_copy(og.at[i, l], ybuf.at[i, l], lsem.at[l * refresh + i]) for i in range(refresh)]
        for l in range(layers)
    ]
    gcopy = pltpu.make_async_copy(gw, gbuf, lsem.at[layers * refresh])
    fcopy = pltpu.make_async_copy(fa, fbuf, lsem.at[layers * refresh + 1])
    for group in copies:
        for cp in group:
            cp.start()
    gcopy.start()
    fcopy.start()

    sides = [xh * nz, (1 - xh) * nz]
    order, origin = [], []
    for j in range(nz):
        k = nz // 2 + (j + 1) // 2 * (1 - 2 * (j % 2))
        there, back = lax.rem(z + k, nz), lax.rem(z + nz - k, nz)
        order += [sides[1] + there, sides[0] + there]
        origin += [sides[1] + back, sides[0] + back]
    peers = [(q * 2 + core, t) for q in order[:others]]
    tpeers = [(dp, lax.rem(t + k, nt)) for k in range(1, nt)]

    barrier = pltpu.get_barrier_semaphore()
    for peer in peers + tpeers + [mate]:
        pl.semaphore_signal(barrier, inc=1, device_id=peer, device_id_type=MESH)

    def send(n, src, dst, peer):
        return pltpu.make_async_remote_copy(
            src_ref=src, dst_ref=dst, send_sem=ssem.at[n], recv_sem=rsem.at[n],
            device_id=peer, device_id_type=MESH,
        )

    weights = [
        (1.0 - AVERAGE_DECAY) * AVERAGE_DECAY ** (refresh - 1 - i) / entries[0] for i in range(refresh)
    ]
    for l in range(layers):
        for cp in copies[l]:
            cp.wait()
        for p in range(per_layer // 2):
            total = None
            for i in range(refresh):
                y = ybuf[i, l, :, wide * p : wide * (p + 1)]
                part = weights[i] * lax.dot_general(
                    y, y, (((0,), (0,)), ((), ())), preferred_element_type=F32
                )
                total = part if total is None else total + part
            pack_pair(total, gram, dgram, l * per_layer + 2 * p)

    def arrange(body, diag, mine, away, dmine, daway):
        for i in range(chips):
            b = table[2 * order[i] + core]
            mine[i] = body[b]
            dmine[i] = diag[b]
            b = table[2 * order[i] + 1 - core]
            away[i] = body[b].astype(BF16)
            daway[i] = diag[b]

    def reduce_scatter(n, mine, away, recv, total, got, dmine, daway, drecv, dtotal, dgot):
        swap = [send(n, away, recv, mate), send(n + 1, daway, drecv, mate)]
        for cp in swap:
            cp.start()
        for cp in swap:
            cp.wait_recv()
        own = mine[others] + recv[others].astype(F32)
        down = dmine[others] + drecv[others]
        total[...] = (mine[:others] + recv[:others].astype(F32)).astype(BF16)
        dtotal[...] = dmine[:others] + drecv[:others]
        for i in range(others):
            send(n + 2, total.at[i], got.at[i], peers[i]).start()
            send(n + 3, dtotal.at[i], dgot.at[i], peers[i]).start()
        whole = [send(n + 2, total, got, mate), send(n + 3, dtotal, dgot, mate)]
        return own, down, swap, whole

    def collect(own, down, whole, got, dgot):
        for cp in whole:
            cp.wait_recv()
        return own + jnp.sum(got[...].astype(F32), axis=0), down + jnp.sum(dgot[...], axis=0)

    arrange(gram, dgram, amine, asend, admine, adsend)
    pl.semaphore_wait(barrier, others + nt)
    own, down, aswap, awhole = reduce_scatter(
        0, amine, asend, arecv, asum, agot, admine, adsend, adrecv, adsum, adgot
    )

    gcopy.wait()
    for l in range(layers):
        for p in range(per_layer // 2):
            g = gbuf[l, :, wide * p : wide * (p + 1)]
            total = lax.dot_general(g, g, (((0,), (0,)), ((), ())), preferred_element_type=F32)
            pack_pair(total, hess, dhess, l * per_layer + 2 * p)
    arrange(hess, dhess, hmine, hsend, hdmine, hdsend)
    hown, hdown, hswap, hwhole = reduce_scatter(
        4, hmine, hsend, hrecv, hsum, hgot, hdmine, hdsend, hdrecv, hdsum, hdgot
    )
    lane = iota(pos_v.shape, 1)
    place = jnp.zeros(pos_v.shape, jnp.int32)
    for j in range(slots):
        owner = core if j < chips else 1 - core
        place = jnp.where(lane == table[2 * origin[j % chips] + owner], j, place)
    pos_v[...] = place
    pcopy = pltpu.make_async_copy(pos_v, pos, lsem.at[layers * refresh + 2])
    pcopy.start()
    pcopy.wait()
    fcopy.wait()

    body, diag = collect(own, down, awhole, agot, adgot)
    fresh = AVERAGE_DECAY**refresh * fbuf[0] + unpack(body, diag)
    fresh_o[0] = fresh
    on = iota((size, size), 0) == iota((size, size), 1)
    inverse = newton_schulz(fresh + jnp.where(on, DAMPING, 0.0))
    xbody, xdiag = pack_one(inverse)
    xbody, xdiag = xbody.astype(BF16), xdiag.astype(BF16).astype(F32)
    xs[...] = xbody
    xd[...] = xdiag
    xall[others] = xbody
    xdall[others] = xdiag
    for i in range(others):
        send(8, xs, xall.at[i], peers[i]).start()
        send(9, xd, xdall.at[i], peers[i]).start()

    hbody, hdiag = collect(hown, hdown, hwhole, hgot, hdgot)
    lane = iota((quarter, wide), 1)
    row = iota((quarter, wide), 0)
    local = jnp.where(lane < size, lane, lane - size - quarter)
    twice = jnp.where(local == row, 0.0, 2.0)
    once = jnp.where(iota((1, wide), 1) < size, xdiag * hdiag, 0.0)
    partial = jnp.sum(twice * xbody.astype(F32) * hbody, axis=0, keepdims=True) + once
    inn[0] = partial
    for k in range(nt - 1):
        send(10, inn.at[0], tin.at[k], tpeers[k]).start()
    tin_all = pltpu.make_async_remote_copy(
        src_ref=tin, dst_ref=tin, send_sem=ssem.at[10], recv_sem=rsem.at[10],
        device_id=mate, device_id_type=MESH,
    )
    tin_all.wait_recv()
    partial = partial + jnp.sum(tin[...], axis=0)
    inn[1] = partial
    for i in range(others):
        send(11, inn.at[1], xin.at[i], peers[i]).start()

    direct = xall.at[pl.ds(0, others)]
    ddirect = xdall.at[pl.ds(0, others)]
    xwhole = [send(8, direct, direct, mate), send(9, ddirect, ddirect, mate)]
    for cp in xwhole:
        cp.wait_recv()
    near, far = pl.ds(0, chips), pl.ds(chips, chips)
    forward = [
        send(12, xall.at[near], xall.at[far], mate),
        send(13, xdall.at[near], xdall.at[far], mate),
    ]
    for cp in forward:
        cp.start()
    xin_all = send(11, xin, xin, mate)
    xin_all.wait_recv()
    partial = partial + jnp.sum(xin[...], axis=0)
    inn[2] = partial
    ccopy = send(14, inn.at[2], cin, mate)
    ccopy.start()
    for cp in forward:
        cp.wait_recv()
    ccopy.wait_recv()
    inner = jnp.sum(partial + cin[...], axis=1, keepdims=True)
    clip = jnp.minimum(1.0, jnp.sqrt(KL_CLIP * entries[1] / inner))

    half = size // 2
    row, lane = iota((half, size), 0), iota((half, size), 1)

    def apply(b, g):
        q = pos[0, b]
        x = xall[q].astype(F32)
        d = 0.5 * xdall[q][:, :size]
        rows = jnp.concatenate([x[:, :size], x[:, size:]], axis=0)
        top = jnp.where(lane > row, rows, jnp.where(lane == row, d, 0.0))
        moved = jnp.concatenate([rows[:, half:], rows[:, :half]], axis=1)
        low = jnp.where(
            (lane >= half) & (lane - half < row), moved, jnp.where(lane - half == row, d, 0.0)
        )
        v = jnp.concatenate([top, low], axis=0).astype(BF16)
        out = jnp.dot(g, v, preferred_element_type=F32)
        out = out + lax.dot_general(g, v, (((1,), (1,)), ((), ())), preferred_element_type=F32)
        return out.astype(BF16).astype(F32)

    for l in range(layers):
        for p in range(per_layer // 2):
            b = l * per_layer + 2 * p
            g = gbuf[l, :, wide * p : wide * (p + 1)]
            out = jnp.concatenate([apply(b, g[:, :size]), apply(b + 1, g[:, size:])], axis=1)
            update_o[l, :, wide * p : wide * (p + 1)] = (clip * out).astype(BF16)

    for cp in aswap + awhole + hswap + hwhole + forward + [ccopy]:
        cp.wait_send()
    for i in range(others):
        send(8, xs, xall.at[i], peers[i]).wait_send()
        send(9, xd, xdall.at[i], peers[i]).wait_send()
        send(11, inn.at[1], xin.at[i], peers[i]).wait_send()
    for k in range(nt - 1):
        send(10, inn.at[0], tin.at[k], tpeers[k]).wait_send()


def finish_kernel(update, fresh, update_o, fresh_o):
    update_o[...] = update[...]
    fresh_o[...] = fresh[...]


def shards(out_grads, grad_w, factor_avg, owner_table):
    refresh, layers, tokens, columns = out_grads.shape
    _, size, _ = factor_avg.shape
    rows = grad_w.shape[1]
    slots = owner_table.shape[0]
    n_dp = lax.axis_size("dp")
    nt = lax.axis_size("tensor")
    nz = n_dp // 4
    chips = slots // 2
    others = chips - 1
    quarter, wide = size // 4, 2 * size
    entries = (float(tokens * n_dp), float(layers * rows * n_dp * columns * nt))
    hbm = pl.BlockSpec(memory_space=pltpu.HBM)
    vmem = pl.BlockSpec(memory_space=pltpu.VMEM)
    smem = pl.BlockSpec(memory_space=pltpu.SMEM)

    def body(n, dtype):
        return pltpu.VMEM((n, quarter, wide), dtype)

    def line(n):
        return pltpu.VMEM((n, 1, wide), F32)

    buffers = [
        body(chips, F32), body(chips, BF16), body(chips, BF16), body(others, BF16), body(others, BF16),
        line(chips), line(chips), line(chips), line(others), line(others),
    ]
    results = (
        jax.ShapeDtypeStruct(grad_w.shape, BF16),
        jax.ShapeDtypeStruct(factor_avg.shape, F32),
    )
    update, fresh = pl.pallas_call(
        functools.partial(exchange_kernel, nz, nt, entries),
        out_shape=results,
        in_specs=[smem, hbm, hbm, hbm],
        out_specs=(vmem, vmem),
        scratch_shapes=[
            pltpu.VMEM(out_grads.shape, BF16),
            pltpu.VMEM(grad_w.shape, BF16),
            pltpu.VMEM(factor_avg.shape, F32),
            body(slots, F32), line(slots), body(slots, F32), line(slots),
            pltpu.VMEM((8, 128), jnp.int32),
            pltpu.SMEM((8, 128), jnp.int32),
            *buffers,
            *buffers,
            pltpu.VMEM((quarter, wide), BF16),
            pltpu.VMEM((1, wide), F32),
            body(slots, BF16), line(slots),
            line(3), line(nt - 1), line(others), pltpu.VMEM((1, wide), F32),
            pltpu.SemaphoreType.DMA((layers * refresh + 3,)),
            pltpu.SemaphoreType.DMA((15,)),
            pltpu.SemaphoreType.DMA((15,)),
        ],
        compiler_params=pltpu.CompilerParams(
            collective_id=0, has_side_effects=True, vmem_limit_bytes=VMEM_KIB * 1024
        ),
        name="exchange",
    )(owner_table, out_grads, grad_w, factor_avg)
    return pl.pallas_call(
        finish_kernel,
        out_shape=results,
        in_specs=[vmem, vmem],
        out_specs=(vmem, vmem),
        name="finish",
    )(update, fresh)


VMEM_KIB = 63 * 1024 + 640


def solution(mesh):
    placed = (
        P(None, None, "dp", "tensor"),
        P(None, "dp", "tensor"),
        P(("dp", "tensor"), None, None),
        P(),
    )
    return jax.shard_map(
        shards,
        mesh=mesh,
        in_specs=placed,
        out_specs=(P(None, "dp", "tensor"), P(("dp", "tensor"), None, None)),
        check_vma=False,
    )
```

```python
import functools

import jax
import jax.numpy as jnp
from jax import lax
from jax.experimental import pallas as pl
from jax.experimental.pallas import tpu as pltpu
from jax.sharding import PartitionSpec as P

STEPS = 8
AVERAGE_DECAY = 0.75
DAMPING = 0.003
KL_CLIP = 0.1
MESH = pl.DeviceIdType.MESH
F32 = jnp.float32
BF16 = jnp.bfloat16


def iota(shape, axis):
    return lax.broadcasted_iota(jnp.int32, shape, axis)


def newton_schulz(damped):
    size = damped.shape[0]
    identity = jnp.where(iota((size, size), 0) == iota((size, size), 1), 1.0, 0.0).astype(F32)

    def dot(a, b):
        return jnp.dot(a, b, precision=lax.Precision.HIGHEST, preferred_element_type=F32)

    scale = 1.0 / jnp.max(jnp.sum(jnp.abs(damped), axis=1, keepdims=True), axis=0, keepdims=True)
    error = identity - scale * damped
    inverse = scale * (identity + error)
    for _ in range(1, STEPS):
        error = dot(error, error)
        inverse = inverse + dot(error, inverse)
    return inverse


def pack_pair(total, body, diag, b):
    wide = total.shape[0]
    size, half, quarter = wide // 2, wide // 4, wide // 8
    row, lane = iota((half, wide), 0), iota((half, wide), 1)
    first = lane < size
    local = jnp.where(first, lane, lane - size)
    upper = jnp.where(first, total[:half], total[size : size + half])
    lower = jnp.where(first, total[half:size], total[size + half :])
    moved = pltpu.roll(lower, wide - half, 1)
    both = jnp.where((local < half) & (row > local), moved, upper)
    turned = pltpu.roll(both, size, 1)
    side = iota((quarter, wide), 1) < size
    body[b] = jnp.where(side, both[:quarter], turned[quarter:])
    body[b + 1] = jnp.where(side, turned[:quarter], both[quarter:])
    on = jnp.where(row == local, upper, 0.0) + jnp.where(row + half == local, lower, 0.0)
    on = jnp.sum(on, axis=0, keepdims=True)
    swapped = pltpu.roll(on, size, 1)
    side = iota((1, wide), 1) < size
    diag[b] = jnp.where(side, on, swapped)
    diag[b + 1] = jnp.where(side, swapped, on)


def unpack(body, diag):
    quarter, wide = body.shape
    size, half = wide // 2, wide // 4
    rows = jnp.concatenate([body[:, :size], body[:, size:]], axis=0)
    corner, side = rows[:, :half], rows[:, half:]
    turned = corner.T
    row, col = iota((half, half), 0), iota((half, half), 1)
    first = jnp.where(col > row, corner, turned)
    last = jnp.where(col < row, corner, turned)
    whole = jnp.concatenate(
        [jnp.concatenate([first, side], axis=1), jnp.concatenate([side.T, last], axis=1)], axis=0
    )
    return jnp.where(iota((size, size), 0) == iota((size, size), 1), diag[:, :size], whole)


def pack_one(whole):
    size = whole.shape[0]
    half, quarter = size // 2, size // 4
    row, col = iota((half, half), 0), iota((half, half), 1)
    corner = jnp.where(row > col, whole[half:, half:], whole[:half, :half])
    rows = jnp.concatenate([corner, whole[:half, half:]], axis=1)
    body = jnp.concatenate([rows[:quarter], rows[quarter:]], axis=1)
    on = jnp.where(iota((size, size), 0) == iota((size, size), 1), whole, 0.0)
    on = jnp.sum(on, axis=0, keepdims=True)
    return body, jnp.concatenate([on, on], axis=1)


def exchange_kernel(
    nz, nt, entries, owners, og, gw, fa, update_o, fresh_o,
    table, ybuf, gbuf, fbuf, gram, dgram, hess, dhess, pos_v, pos,
    amine, asend, arecv, asum, agot, admine, adsend, adrecv, adsum, adgot,
    hmine, hsend, hrecv, hsum, hgot, hdmine, hdsend, hdrecv, hdsum, hdgot,
    hleave, hacross, hdacross, xs, xd, xall, xdall, inn, pin, zin, pre, lsem, ssem, rsem,
):
    refresh, layers, tokens, columns = ybuf.shape
    slots, quarter, wide = gram.shape
    size = wide // 2
    per_layer = columns // size
    chips = slots // 2
    others = chips - 1
    dp = lax.axis_index("dp")
    t = lax.axis_index("tensor")
    core = lax.rem(dp, 2)
    here = lax.div(dp, 2)
    xh = lax.div(here, nz)
    z = lax.rem(here, nz)
    mate = (dp + 1 - 2 * core, t)

    copies = [
        [pltpu.make_async_copy(og.at[i, l], ybuf.at[i, l], lsem.at[l * refresh + i]) for i in range(refresh)]
        for l in range(layers)
    ]
    tcopy = pltpu.make_async_copy(owners, table, lsem.at[layers * refresh + 3])
    gcopy = pltpu.make_async_copy(gw, gbuf, lsem.at[layers * refresh])
    fcopy = pltpu.make_async_copy(fa, fbuf, lsem.at[layers * refresh + 1])
    sides = [xh * nz, (1 - xh) * nz]
    steps = [nz // 2 + (j + 1) // 2 * (1 - 2 * (j % 2)) for j in range(nz)]
    there = [lax.rem(z + k, nz) for k in steps]
    back = [lax.rem(z + nz - k, nz) for k in steps]
    order = [sides[1] + q for q in there] + [sides[0] + q for q in there]
    origin = [sides[1] + q for q in back] + [sides[0] + q for q in back]
    peers = [(q * 2 + core, t) for q in order[:others]]
    issue = [i for j in range(nz) for i in (j, nz + j) if i < others]
    across = peers[nz - 1]
    zpeers = peers[nz:]
    plane = []
    for a in range(2):
        for c in range(2):
            for k in range(nt):
                if a + c + k:
                    plane.append(
                        ((sides[a] + z) * 2 + (core if c == 0 else 1 - core), lax.rem(t + k, nt))
                    )
    greeted = [peers[i] for i in issue]
    greeted += [p for n, p in enumerate(plane) if n + 1 not in (nt, 2 * nt)] + [mate]

    barrier = pltpu.get_barrier_semaphore()
    for peer in greeted:
        pl.semaphore_signal(barrier, inc=1, device_id=peer, device_id_type=MESH)
    tcopy.start()
    gcopy.start()
    for group in copies:
        for cp in group:
            cp.start()
    fcopy.start()

    def send(n, src, dst, peer):
        return pltpu.make_async_remote_copy(
            src_ref=src, dst_ref=dst, send_sem=ssem.at[n], recv_sem=rsem.at[n],
            device_id=peer, device_id_type=MESH,
        )

    gcopy.wait()
    for l in range(layers):
        for p in range(per_layer // 2):
            g = gbuf[l, :, wide * p : wide * (p + 1)]
            total = lax.dot_general(g, g, (((0,), (0,)), ((), ())), preferred_element_type=F32)
            pack_pair(total, hess, dhess, l * per_layer + 2 * p)

    weights = [
        (1.0 - AVERAGE_DECAY) * AVERAGE_DECAY ** (refresh - 1 - i) / entries[0] for i in range(refresh)
    ]
    for l in range(layers):
        for cp in copies[l]:
            cp.wait()
        for p in range(per_layer // 2):
            total = None
            for i in range(refresh):
                y = ybuf[i, l, :, wide * p : wide * (p + 1)]
                part = weights[i] * lax.dot_general(
                    y, y, (((0,), (0,)), ((), ())), preferred_element_type=F32
                )
                total = part if total is None else total + part
            pack_pair(total, gram, dgram, l * per_layer + 2 * p)

    def arrange(body, diag, mine, away, dmine, daway):
        for i in range(chips):
            b = table[2 * order[i] + core]
            mine[i] = body[b]
            dmine[i] = diag[b]
            b = table[2 * order[i] + 1 - core]
            away[i] = body[b].astype(BF16)
            daway[i] = diag[b]

    tcopy.wait()
    arrange(gram, dgram, amine, asend, admine, adsend)
    arrange(hess, dhess, hmine, hsend, hdmine, hdsend)
    pl.semaphore_wait(barrier, len(greeted))

    aswap = [send(0, asend, arecv, mate), send(1, adsend, adrecv, mate)]
    hswap = [send(2, hsend, hrecv, mate), send(3, hdsend, hdrecv, mate)]
    for cp in aswap + hswap:
        cp.start()

    for cp in aswap:
        cp.wait_recv()
    asum[...] = (amine[:others] + arecv[:others].astype(F32)).astype(BF16)
    adsum[...] = admine[:others] + adrecv[:others]
    for i in issue:
        send(4, asum.at[i], agot.at[i], peers[i]).start()
        send(5, adsum.at[i], adgot.at[i], peers[i]).start()

    for cp in hswap:
        cp.wait_recv()
    hmine[...] = hmine[...] + hrecv[...].astype(F32)
    hdmine[...] = hdmine[...] + hdrecv[...]
    hleave[...] = hmine[:nz].astype(BF16)
    xswap = [
        send(6, hleave, hacross, across),
        send(7, hdmine.at[pl.ds(0, nz)], hdacross, across),
    ]
    for cp in xswap:
        cp.start()

    lane = iota(pos_v.shape, 1)
    place = jnp.zeros(pos_v.shape, jnp.int32)
    for j in range(slots):
        owner = core if j < chips else 1 - core
        place = jnp.where(lane == table[2 * origin[j % chips] + owner], j, place)
    pos_v[...] = place
    pcopy = pltpu.make_async_copy(pos_v, pos, lsem.at[layers * refresh + 2])
    pcopy.start()
    for cp in xswap:
        cp.wait_recv()
    hmine[nz:] = hmine[nz:] + hacross[...].astype(F32)
    hdmine[nz:] = hdmine[nz:] + hdacross[...]
    hsum[...] = hmine[nz:others].astype(BF16)
    hdsum[...] = hdmine[nz:others]
    for i in range(nz - 1):
        send(8, hsum.at[i], hgot.at[i], zpeers[i]).start()
        send(9, hdsum.at[i], hdgot.at[i], zpeers[i]).start()
    pcopy.wait()
    fcopy.wait()

    awhole = [send(4, asum, agot, mate), send(5, adsum, adgot, mate)]
    for cp in awhole:
        cp.wait_recv()
    body = amine[others] + arecv[others].astype(F32) + jnp.sum(agot[...].astype(F32), axis=0)
    diag = admine[others] + adrecv[others] + jnp.sum(adgot[...], axis=0)
    fresh = AVERAGE_DECAY**refresh * fbuf[0] + unpack(body, diag)
    fresh_o[0] = fresh
    on = iota((size, size), 0) == iota((size, size), 1)
    inverse = newton_schulz(fresh + jnp.where(on, DAMPING, 0.0))
    xbody, xdiag = pack_one(inverse)
    xbody, xdiag = xbody.astype(BF16), xdiag.astype(BF16).astype(F32)
    xs[...] = xbody
    xd[...] = xdiag
    xall[others] = xbody
    xdall[others] = xdiag
    for i in issue:
        send(10, xs, xall.at[i], peers[i]).start()
        send(11, xd, xdall.at[i], peers[i]).start()

    hwhole = [send(8, hsum, hgot, mate), send(9, hdsum, hdgot, mate)]
    for cp in hwhole:
        cp.wait_recv()
    hbody = hmine[others] + jnp.sum(hgot[...].astype(F32), axis=0)
    hdiag = hdmine[others] + jnp.sum(hdgot[...], axis=0)
    lane = iota((quarter, wide), 1)
    row = iota((quarter, wide), 0)
    local = jnp.where(lane < size, lane, lane - size - quarter)
    twice = jnp.where(local == row, 0.0, 2.0)
    once = jnp.where(iota((1, wide), 1) < size, xdiag * hdiag, 0.0)
    partial = jnp.sum(twice * xbody.astype(F32) * hbody, axis=0, keepdims=True) + once
    inn[0] = partial
    for n, peer in enumerate(plane):
        send(12, inn.at[0], pin.at[n], peer).start()
    pin_all = send(12, pin, pin, mate)
    pin_all.wait_recv()
    partial = partial + jnp.sum(pin[...], axis=0)
    inn[1] = partial
    for i in range(nz - 1):
        send(13, inn.at[1], zin.at[i], zpeers[i]).start()

    direct, ddirect = xall.at[pl.ds(0, others)], xdall.at[pl.ds(0, others)]
    xwhole = [send(10, direct, direct, mate), send(11, ddirect, ddirect, mate)]
    for cp in xwhole:
        cp.wait_recv()
    near, far = pl.ds(0, chips), pl.ds(chips, chips)
    forward = [
        send(14, xall.at[near], xall.at[far], mate),
        send(15, xdall.at[near], xdall.at[far], mate),
    ]
    for cp in forward:
        cp.start()
    for cp in forward:
        cp.wait_recv()

    half = size // 2
    row, lane = iota((half, size), 0), iota((half, size), 1)

    def apply(b, g):
        q = pos[0, b]
        x = xall[q].astype(F32)
        d = 0.5 * xdall[q][:, :size]
        rows = jnp.concatenate([x[:, :size], x[:, size:]], axis=0)
        top = jnp.where(lane > row, rows, jnp.where(lane == row, d, 0.0))
        moved = jnp.concatenate([rows[:, half:], rows[:, :half]], axis=1)
        low = jnp.where(
            (lane >= half) & (lane - half < row), moved, jnp.where(lane - half == row, d, 0.0)
        )
        v = jnp.concatenate([top, low], axis=0).astype(BF16)
        out = jnp.dot(g, v, preferred_element_type=F32)
        out = out + lax.dot_general(g, v, (((1,), (1,)), ((), ())), preferred_element_type=F32)
        return out.astype(BF16)

    for l in range(layers):
        for p in range(per_layer // 2):
            b = l * per_layer + 2 * p
            g = gbuf[l, :, wide * p : wide * (p + 1)]
            out = jnp.concatenate([apply(b, g[:, :size]), apply(b + 1, g[:, size:])], axis=1)
            pre[l, :, wide * p : wide * (p + 1)] = out

    for cp in aswap + awhole + hswap + xswap + hwhole + xwhole + forward + [pin_all]:
        cp.wait_send()
    zin_all = send(13, zin, zin, mate)
    zin_all.wait_recv()
    partial = partial + jnp.sum(zin[...], axis=0)
    inner = jnp.sum(partial, axis=1, keepdims=True)
    clip = jnp.minimum(1.0, jnp.sqrt(KL_CLIP * entries[1] / inner))
    for l in range(layers):
        update_o[l] = (clip * pre[l].astype(F32)).astype(BF16)

    zin_all.wait_send()


def finish_kernel(update, fresh, update_o, fresh_o, sems):
    copies = [
        pltpu.make_async_copy(update, update_o, sems.at[0]),
        pltpu.make_async_copy(fresh, fresh_o, sems.at[1]),
    ]
    for cp in copies:
        cp.start()
    for cp in copies:
        cp.wait()


def shards(out_grads, grad_w, factor_avg, owner_table):
    refresh, layers, tokens, columns = out_grads.shape
    _, size, _ = factor_avg.shape
    rows = grad_w.shape[1]
    slots = owner_table.shape[0]
    n_dp = lax.axis_size("dp")
    nt = lax.axis_size("tensor")
    nz = n_dp // 4
    chips = slots // 2
    others = chips - 1
    quarter, wide = size // 4, 2 * size
    entries = (float(tokens * n_dp), float(layers * rows * n_dp * columns * nt))
    hbm = pl.BlockSpec(memory_space=pltpu.HBM)
    vmem = pl.BlockSpec(memory_space=pltpu.VMEM)

    def body(n, dtype):
        return pltpu.VMEM((n, quarter, wide), dtype)

    def line(n):
        return pltpu.VMEM((n, 1, wide), F32)

    def buffers(n):
        return [
            body(chips, F32), body(chips, BF16), body(chips, BF16), body(n, BF16), body(n, BF16),
            line(chips), line(chips), line(chips), line(n), line(n),
        ]

    update, fresh = pl.pallas_call(
        functools.partial(exchange_kernel, nz, nt, entries),
        out_shape=(pltpu.VMEM(grad_w.shape, BF16), pltpu.VMEM(factor_avg.shape, F32)),
        in_specs=[hbm, hbm, hbm, hbm],
        out_specs=(vmem, vmem),
        scratch_shapes=[
            pltpu.SMEM(owner_table.shape, jnp.int32),
            pltpu.VMEM(out_grads.shape, BF16),
            pltpu.VMEM(grad_w.shape, BF16),
            pltpu.VMEM(factor_avg.shape, F32),
            body(slots, F32), line(slots), body(slots, F32), line(slots),
            pltpu.VMEM((8, 128), jnp.int32),
            pltpu.SMEM((8, 128), jnp.int32),
            *buffers(others),
            *buffers(nz - 1),
            body(nz, BF16), body(nz, BF16), line(nz),
            pltpu.VMEM((quarter, wide), BF16),
            pltpu.VMEM((1, wide), F32),
            body(slots, BF16), line(slots),
            line(2), line(4 * nt - 1), line(nz - 1),
            pltpu.VMEM(grad_w.shape, BF16),
            pltpu.SemaphoreType.DMA((layers * refresh + 4,)),
            pltpu.SemaphoreType.DMA((16,)),
            pltpu.SemaphoreType.DMA((16,)),
        ],
        compiler_params=pltpu.CompilerParams(
            collective_id=0, has_side_effects=True, vmem_limit_bytes=VMEM_KIB * 1024
        ),
        name="exchange",
    )(owner_table, out_grads, grad_w, factor_avg)
    update = pltpu.with_memory_space_constraint(update, pltpu.VMEM)
    fresh = pltpu.with_memory_space_constraint(fresh, pltpu.VMEM)
    return pl.pallas_call(
        finish_kernel,
        out_shape=(
            jax.ShapeDtypeStruct(grad_w.shape, BF16),
            jax.ShapeDtypeStruct(factor_avg.shape, F32),
        ),
        in_specs=[pl.BlockSpec(memory_space=pl.ANY)] * 2,
        out_specs=[pl.BlockSpec(memory_space=pl.ANY)] * 2,
        scratch_shapes=[pltpu.SemaphoreType.DMA((2,))],
        name="finish",
    )(update, fresh)


VMEM_KIB = 63 * 1024 + 640


def solution(mesh):
    placed = (
        P(None, None, "dp", "tensor"),
        P(None, "dp", "tensor"),
        P(("dp", "tensor"), None, None),
        P(),
    )
    return jax.shard_map(
        shards,
        mesh=mesh,
        in_specs=placed,
        out_specs=(P(None, "dp", "tensor"), P(("dp", "tensor"), None, None)),
        check_vma=False,
    )
```

```python
import functools

import jax
import jax.numpy as jnp
from jax import lax
from jax.experimental import pallas as pl
from jax.experimental.pallas import tpu as pltpu
from jax.sharding import PartitionSpec as P

STEPS = 8
AVERAGE_DECAY = 0.75
DAMPING = 0.003
KL_CLIP = 0.1
MESH = pl.DeviceIdType.MESH
F32 = jnp.float32
BF16 = jnp.bfloat16


def iota(shape, axis):
    return lax.broadcasted_iota(jnp.int32, shape, axis)


def newton_schulz(damped):
    size = damped.shape[0]
    identity = jnp.where(iota((size, size), 0) == iota((size, size), 1), 1.0, 0.0).astype(F32)

    def dot(a, b):
        return jnp.dot(a, b, precision=lax.Precision.HIGHEST, preferred_element_type=F32)

    scale = 1.0 / jnp.max(jnp.sum(jnp.abs(damped), axis=1, keepdims=True), axis=0, keepdims=True)
    error = identity - scale * damped
    inverse = scale * (identity + error)
    for _ in range(1, STEPS):
        error = dot(error, error)
        inverse = inverse + dot(error, inverse)
    return inverse


def pack_pair(total, body, diag, b):
    wide = total.shape[0]
    size, half, quarter = wide // 2, wide // 4, wide // 8
    row, lane = iota((half, wide), 0), iota((half, wide), 1)
    first = lane < size
    local = jnp.where(first, lane, lane - size)
    upper = jnp.where(first, total[:half], total[size : size + half])
    lower = jnp.where(first, total[half:size], total[size + half :])
    moved = pltpu.roll(lower, wide - half, 1)
    both = jnp.where((local < half) & (row > local), moved, upper)
    turned = pltpu.roll(both, size, 1)
    side = iota((quarter, wide), 1) < size
    body[b] = jnp.where(side, both[:quarter], turned[quarter:])
    body[b + 1] = jnp.where(side, turned[:quarter], both[quarter:])
    on = jnp.where(row == local, upper, 0.0) + jnp.where(row + half == local, lower, 0.0)
    on = jnp.sum(on, axis=0, keepdims=True)
    swapped = pltpu.roll(on, size, 1)
    side = iota((1, wide), 1) < size
    diag[b] = jnp.where(side, on, swapped)
    diag[b + 1] = jnp.where(side, swapped, on)


def unpack(body, diag):
    quarter, wide = body.shape
    size, half = wide // 2, wide // 4
    rows = jnp.concatenate([body[:, :size], body[:, size:]], axis=0)
    corner, side = rows[:, :half], rows[:, half:]
    turned = corner.T
    row, col = iota((half, half), 0), iota((half, half), 1)
    first = jnp.where(col > row, corner, turned)
    last = jnp.where(col < row, corner, turned)
    whole = jnp.concatenate(
        [jnp.concatenate([first, side], axis=1), jnp.concatenate([side.T, last], axis=1)], axis=0
    )
    return jnp.where(iota((size, size), 0) == iota((size, size), 1), diag[:, :size], whole)


def pack_one(whole):
    size = whole.shape[0]
    half, quarter = size // 2, size // 4
    row, col = iota((half, half), 0), iota((half, half), 1)
    corner = jnp.where(row > col, whole[half:, half:], whole[:half, :half])
    rows = jnp.concatenate([corner, whole[:half, half:]], axis=1)
    body = jnp.concatenate([rows[:quarter], rows[quarter:]], axis=1)
    on = jnp.where(iota((size, size), 0) == iota((size, size), 1), whole, 0.0)
    on = jnp.sum(on, axis=0, keepdims=True)
    return body, jnp.concatenate([on, on], axis=1)


def exchange_kernel(
    nz, nt, entries, owners, og, gw, fa, update_o, fresh_o,
    table, ybuf, gbuf, fbuf, gram, dgram, hess, dhess, pos_v, pos,
    amine, asend, arecv, asum, agot, dmine, dsend, drecv, dsum, dgot,
    hmine, hsend, hrecv, hsum, hgot, hleave, hacross, xs, xd, xall, xdall, inn, pin, zin, pre, lsem, ssem, rsem,
):
    refresh, layers, tokens, columns = ybuf.shape
    slots, quarter, wide = gram.shape
    size = wide // 2
    per_layer = columns // size
    chips = slots // 2
    others = chips - 1
    dp = lax.axis_index("dp")
    t = lax.axis_index("tensor")
    core = lax.rem(dp, 2)
    here = lax.div(dp, 2)
    xh = lax.div(here, nz)
    z = lax.rem(here, nz)
    mate = (dp + 1 - 2 * core, t)

    copies = [
        [pltpu.make_async_copy(og.at[i, l], ybuf.at[i, l], lsem.at[l * refresh + i]) for i in range(refresh)]
        for l in range(layers)
    ]
    tcopy = pltpu.make_async_copy(owners, table, lsem.at[layers * refresh + 3])
    gcopy = pltpu.make_async_copy(gw, gbuf, lsem.at[layers * refresh])
    fcopy = pltpu.make_async_copy(fa, fbuf, lsem.at[layers * refresh + 1])
    sides = [xh * nz, (1 - xh) * nz]
    steps = [nz // 2 + (j + 1) // 2 * (1 - 2 * (j % 2)) for j in range(nz)]
    there = [lax.rem(z + k, nz) for k in steps]
    back = [lax.rem(z + nz - k, nz) for k in steps]
    order = [sides[1] + q for q in there] + [sides[0] + q for q in there]
    origin = [sides[1] + q for q in back] + [sides[0] + q for q in back]
    peers = [(q * 2 + core, t) for q in order[:others]]
    issue = [i for j in range(nz) for i in (j, nz + j) if i < others]
    across = peers[nz - 1]
    zpeers = peers[nz:]
    plane = []
    for a in range(2):
        for c in range(2):
            for k in range(nt):
                if a + c + k:
                    plane.append(
                        ((sides[a] + z) * 2 + (core if c == 0 else 1 - core), lax.rem(t + k, nt))
                    )
    greeted = [peers[i] for i in issue]
    greeted += [p for n, p in enumerate(plane) if n + 1 not in (nt, 2 * nt)] + [mate]

    barrier = pltpu.get_barrier_semaphore()
    for peer in greeted:
        pl.semaphore_signal(barrier, inc=1, device_id=peer, device_id_type=MESH)
    tcopy.start()
    gcopy.start()
    for group in copies:
        for cp in group:
            cp.start()
    fcopy.start()

    def send(n, src, dst, peer):
        return pltpu.make_async_remote_copy(
            src_ref=src, dst_ref=dst, send_sem=ssem.at[n], recv_sem=rsem.at[n],
            device_id=peer, device_id_type=MESH,
        )

    gcopy.wait()
    for l in range(layers):
        for p in range(per_layer // 2):
            g = gbuf[l, :, wide * p : wide * (p + 1)]
            total = lax.dot_general(g, g, (((0,), (0,)), ((), ())), preferred_element_type=F32)
            pack_pair(total, hess, dhess, l * per_layer + 2 * p)

    weights = [
        (1.0 - AVERAGE_DECAY) * AVERAGE_DECAY ** (refresh - 1 - i) / entries[0] for i in range(refresh)
    ]
    for l in range(layers):
        for cp in copies[l]:
            cp.wait()
        for p in range(per_layer // 2):
            total = None
            for i in range(refresh):
                y = ybuf[i, l, :, wide * p : wide * (p + 1)]
                part = weights[i] * lax.dot_general(
                    y, y, (((0,), (0,)), ((), ())), preferred_element_type=F32
                )
                total = part if total is None else total + part
            pack_pair(total, gram, dgram, l * per_layer + 2 * p)

    tcopy.wait()
    left = iota((1, wide), 1) < size
    for i in range(chips):
        b = table[2 * order[i] + core]
        amine[i] = gram[b]
        hmine[i] = hess[b]
        dmine[i] = jnp.where(left, dgram[b], dhess[b])
        b = table[2 * order[i] + 1 - core]
        asend[i] = gram[b].astype(BF16)
        hsend[i] = hess[b].astype(BF16)
        dsend[i] = jnp.where(left, dgram[b], dhess[b])
    pl.semaphore_wait(barrier, len(greeted))

    aswap = [send(0, asend, arecv, mate), send(1, dsend, drecv, mate)]
    hswap = [send(2, hsend, hrecv, mate)]
    for cp in aswap + hswap:
        cp.start()

    for cp in aswap:
        cp.wait_recv()
    asum[...] = (amine[:others] + arecv[:others].astype(F32)).astype(BF16)
    dsum[...] = dmine[:others] + drecv[:others]
    for i in issue:
        send(4, asum.at[i], agot.at[i], peers[i]).start()
        send(5, dsum.at[i], dgot.at[i], peers[i]).start()

    for cp in hswap:
        cp.wait_recv()
    hmine[...] = hmine[...] + hrecv[...].astype(F32)
    hleave[...] = hmine[:nz].astype(BF16)
    xswap = [send(6, hleave, hacross, across)]
    for cp in xswap:
        cp.start()

    lane = iota(pos_v.shape, 1)
    place = jnp.zeros(pos_v.shape, jnp.int32)
    for j in range(slots):
        owner = core if j < chips else 1 - core
        place = jnp.where(lane == table[2 * origin[j % chips] + owner], j, place)
    pos_v[...] = place
    pcopy = pltpu.make_async_copy(pos_v, pos, lsem.at[layers * refresh + 2])
    pcopy.start()
    for cp in xswap:
        cp.wait_recv()
    hmine[nz:] = hmine[nz:] + hacross[...].astype(F32)
    hsum[...] = hmine[nz:others].astype(BF16)
    for i in range(nz - 1):
        send(8, hsum.at[i], hgot.at[i], zpeers[i]).start()
    pcopy.wait()
    fcopy.wait()

    awhole = [send(4, asum, agot, mate), send(5, dsum, dgot, mate)]
    for cp in awhole:
        cp.wait_recv()
    body = amine[others] + arecv[others].astype(F32) + jnp.sum(agot[...].astype(F32), axis=0)
    diag = dmine[others] + drecv[others] + jnp.sum(dgot[...], axis=0)
    fresh = AVERAGE_DECAY**refresh * fbuf[0] + unpack(body, diag)
    fresh_o[0] = fresh
    on = iota((size, size), 0) == iota((size, size), 1)
    inverse = newton_schulz(fresh + jnp.where(on, DAMPING, 0.0))
    xbody, xdiag = pack_one(inverse)
    xbody, xdiag = xbody.astype(BF16), xdiag.astype(BF16).astype(F32)
    xs[...] = xbody
    xd[...] = xdiag
    xall[others] = xbody
    xdall[others] = xdiag
    for i in issue:
        send(10, xs, xall.at[i], peers[i]).start()
        send(11, xd, xdall.at[i], peers[i]).start()

    hwhole = [send(8, hsum, hgot, mate)]
    for cp in hwhole:
        cp.wait_recv()
    hbody = hmine[others] + jnp.sum(hgot[...].astype(F32), axis=0)
    lane = iota((quarter, wide), 1)
    row = iota((quarter, wide), 0)
    local = jnp.where(lane < size, lane, lane - size - quarter)
    twice = jnp.where(local == row, 0.0, 2.0)
    once = jnp.where(left, 0.0, xdiag * diag)
    partial = jnp.sum(twice * xbody.astype(F32) * hbody, axis=0, keepdims=True) + once
    inn[0] = partial
    for n, peer in enumerate(plane):
        send(12, inn.at[0], pin.at[n], peer).start()
    pin_all = send(12, pin, pin, mate)
    pin_all.wait_recv()
    partial = partial + jnp.sum(pin[...], axis=0)
    inn[1] = partial
    for i in range(nz - 1):
        send(13, inn.at[1], zin.at[i], zpeers[i]).start()

    direct, ddirect = xall.at[pl.ds(0, others)], xdall.at[pl.ds(0, others)]
    xwhole = [send(10, direct, direct, mate), send(11, ddirect, ddirect, mate)]
    for cp in xwhole:
        cp.wait_recv()
    near, far = pl.ds(0, chips), pl.ds(chips, chips)
    forward = [
        send(14, xall.at[near], xall.at[far], mate),
        send(15, xdall.at[near], xdall.at[far], mate),
    ]
    for cp in forward:
        cp.start()
    for cp in forward:
        cp.wait_recv()

    half = size // 2
    row, lane = iota((half, size), 0), iota((half, size), 1)

    def apply(b, g):
        q = pos[0, b]
        x = xall[q].astype(F32)
        d = 0.5 * xdall[q][:, :size]
        rows = jnp.concatenate([x[:, :size], x[:, size:]], axis=0)
        top = jnp.where(lane > row, rows, jnp.where(lane == row, d, 0.0))
        moved = jnp.concatenate([rows[:, half:], rows[:, :half]], axis=1)
        low = jnp.where(
            (lane >= half) & (lane - half < row), moved, jnp.where(lane - half == row, d, 0.0)
        )
        v = jnp.concatenate([top, low], axis=0).astype(BF16)
        out = jnp.dot(g, v, preferred_element_type=F32)
        out = out + lax.dot_general(g, v, (((1,), (1,)), ((), ())), preferred_element_type=F32)
        return out.astype(BF16)

    for l in range(layers):
        for p in range(per_layer // 2):
            b = l * per_layer + 2 * p
            g = gbuf[l, :, wide * p : wide * (p + 1)]
            out = jnp.concatenate([apply(b, g[:, :size]), apply(b + 1, g[:, size:])], axis=1)
            pre[l, :, wide * p : wide * (p + 1)] = out

    for cp in aswap + awhole + hswap + xswap + hwhole + xwhole + forward + [pin_all]:
        cp.wait_send()
    zin_all = send(13, zin, zin, mate)
    zin_all.wait_recv()
    partial = partial + jnp.sum(zin[...], axis=0)
    inner = jnp.sum(partial, axis=1, keepdims=True)
    clip = jnp.minimum(1.0, jnp.sqrt(KL_CLIP * entries[1] / inner))
    for l in range(layers):
        update_o[l] = (clip * pre[l].astype(F32)).astype(BF16)

    zin_all.wait_send()


def finish_kernel(update, fresh, update_o, fresh_o, sems):
    copies = [
        pltpu.make_async_copy(update, update_o, sems.at[0]),
        pltpu.make_async_copy(fresh, fresh_o, sems.at[1]),
    ]
    for cp in copies:
        cp.start()
    for cp in copies:
        cp.wait()


def shards(out_grads, grad_w, factor_avg, owner_table):
    refresh, layers, tokens, columns = out_grads.shape
    _, size, _ = factor_avg.shape
    rows = grad_w.shape[1]
    slots = owner_table.shape[0]
    n_dp = lax.axis_size("dp")
    nt = lax.axis_size("tensor")
    nz = n_dp // 4
    chips = slots // 2
    others = chips - 1
    quarter, wide = size // 4, 2 * size
    entries = (float(tokens * n_dp), float(layers * rows * n_dp * columns * nt))
    hbm = pl.BlockSpec(memory_space=pltpu.HBM)
    vmem = pl.BlockSpec(memory_space=pltpu.VMEM)

    def body(n, dtype):
        return pltpu.VMEM((n, quarter, wide), dtype)

    def line(n):
        return pltpu.VMEM((n, 1, wide), F32)

    def buffers(n):
        return [body(chips, F32), body(chips, BF16), body(chips, BF16), body(n, BF16), body(n, BF16)]

    update, fresh = pl.pallas_call(
        functools.partial(exchange_kernel, nz, nt, entries),
        out_shape=(pltpu.VMEM(grad_w.shape, BF16), pltpu.VMEM(factor_avg.shape, F32)),
        in_specs=[hbm, hbm, hbm, hbm],
        out_specs=(vmem, vmem),
        scratch_shapes=[
            pltpu.SMEM(owner_table.shape, jnp.int32),
            pltpu.VMEM(out_grads.shape, BF16),
            pltpu.VMEM(grad_w.shape, BF16),
            pltpu.VMEM(factor_avg.shape, F32),
            body(slots, F32), line(slots), body(slots, F32), line(slots),
            pltpu.VMEM((8, 128), jnp.int32),
            pltpu.SMEM((8, 128), jnp.int32),
            *buffers(others),
            line(chips), line(chips), line(chips), line(others), line(others),
            *buffers(nz - 1),
            body(nz, BF16), body(nz, BF16),
            pltpu.VMEM((quarter, wide), BF16),
            pltpu.VMEM((1, wide), F32),
            body(slots, BF16), line(slots),
            line(2), line(4 * nt - 1), line(nz - 1),
            pltpu.VMEM(grad_w.shape, BF16),
            pltpu.SemaphoreType.DMA((layers * refresh + 4,)),
            pltpu.SemaphoreType.DMA((16,)),
            pltpu.SemaphoreType.DMA((16,)),
        ],
        compiler_params=pltpu.CompilerParams(
            collective_id=0, has_side_effects=True, vmem_limit_bytes=VMEM_KIB * 1024
        ),
        name="exchange",
    )(owner_table, out_grads, grad_w, factor_avg)
    update = pltpu.with_memory_space_constraint(update, pltpu.VMEM)
    fresh = pltpu.with_memory_space_constraint(fresh, pltpu.VMEM)
    return pl.pallas_call(
        finish_kernel,
        out_shape=(
            jax.ShapeDtypeStruct(grad_w.shape, BF16),
            jax.ShapeDtypeStruct(factor_avg.shape, F32),
        ),
        in_specs=[pl.BlockSpec(memory_space=pl.ANY)] * 2,
        out_specs=[pl.BlockSpec(memory_space=pl.ANY)] * 2,
        scratch_shapes=[pltpu.SemaphoreType.DMA((2,))],
        name="finish",
    )(update, fresh)


VMEM_KIB = 63 * 1024 + 640


def solution(mesh):
    placed = (
        P(None, None, "dp", "tensor"),
        P(None, "dp", "tensor"),
        P(("dp", "tensor"), None, None),
        P(),
    )
    return jax.shard_map(
        shards,
        mesh=mesh,
        in_specs=placed,
        out_specs=(P(None, "dp", "tensor"), P(("dp", "tensor"), None, None)),
        check_vma=False,
    )
```
